32 devices in a mesh: groups: 2 (over x), ex: 16 (over z, y, core).
Axes of the slice: x: 2, y: 2, z: 4, core: 2. Of those that a mesh axis runs over, the one named last changes fastest.
Arguments:
- orbitals: bfloat16 [32768, 1024], P(('groups', 'ex')), parts along dimension 0, may hold values from -6 to 6
- element_blocks: bfloat16 [128, 256, 256], P(('groups', 'ex')), parts along dimension 0, may hold values from -0.25 to 6.75, as said below
- face_couplings: bfloat16 [3, 128, 256, 256], P(None, ('groups', 'ex')), parts along dimension 1, may hold values from -0.119628906 to 0.119628906
- face_order: int32 [3, 64, 256], P(None, 'ex'), may hold values from 0 to 255, each once within a row
Outputs:
- orthonormal: bfloat16 [32768, 1024], P(('groups', 'ex')), parts along dimension 0
The draws below stay inside these ranges and needn't reach their ends.
There are 2 independent parts, one for each index of `groups`. The reference program is written for one: setup_inputs(seed, part) draws one part's arguments, and reference() takes and returns one part's arrays. A program takes and returns all parts, laid end to end along the dimension named above; an argument that names none is the same for every part. Nothing has to cross between parts.
Inputs may be any that keep to these rules, and one draw needn't show every extreme that they name: Each row of face_order names every one of 0 to 255 once. Each block of element_blocks is symmetric.
All inputs are finite; a program needn't handle non-finite values.
Results may differ from the reference program's by a relative error of at most 0.007.
Values may be sent and summed in bfloat16 or wider, within the bound.
A program may use at most 128 MiB of HBM per device.

```python
import jax
import jax.numpy as jnp

NB = 256
NORB = 1024
EY = 2
EZ = 2
NXE = 16
ELEMS = 64
ROWS = 16384


def draw_element_blocks(key, part):
    key = jax.random.fold_in(key, 11)
    first_key, second_key = jax.random.split(key, 2)
    layer = (jnp.arange(ELEMS, dtype=jnp.int32) // (EY * EZ)).astype(jnp.float32)
    position = layer / float(NXE)
    level = 1.5 + 3.0 * position
    rough = jnp.exp(jax.random.uniform(first_key, (ELEMS, NB), jnp.float32, jnp.log(0.7), jnp.log(1.4)))
    noise = jnp.clip(jax.random.normal(second_key, (ELEMS, NB, NB), jnp.float32), -4.0, 4.0)
    diagonal = level[:, None] * rough
    symmetric = (noise + jnp.transpose(noise, (0, 2, 1))) * (1.0 / 32.0)
    identity = jnp.eye(NB, dtype=jnp.float32)
    blocks = symmetric * (1.0 - identity)[None] + diagonal[:, :, None] * identity[None]
    return blocks.astype(jnp.bfloat16)


def steps_of(stream_key, extent, shards, least, largest):
    def one(dim, parts):
        draws = jax.random.uniform(jax.random.fold_in(jax.random.fold_in(stream_key, 6), dim), (parts,), jnp.float32, least / len(shards), largest / len(shards))
        return jnp.repeat(jnp.exp(draws), extent[dim] // parts).reshape((-1,) + (1,) * (len(extent) - dim - 1))

    level = one(*shards[0])
    for cut in shards[1:]:
        level = level * one(*cut)
    return level


def bell_draw(own_key, shape, scale, limit, cuts=(), held_as=jnp.bfloat16):
    result = jax.random.normal(own_key, shape, jnp.float32) * scale
    if len(cuts) > 0:
        result = steps_of(own_key, shape, cuts, -0.22, 0.18) * result
    return jnp.clip(result, min=-limit, max=limit).astype(held_as)


def setup_inputs(seed: int = 0, part: int = 0) -> dict:
    keys = jax.random.split(jax.random.key(seed), 5)
    own_keys = jax.random.split(jax.random.fold_in(keys[4], part), 5)
    orbitals = bell_draw(own_keys[0], (ROWS, NORB), 1.0, 6.0, ((0, 16),))
    element_blocks = draw_element_blocks(jax.random.fold_in(jax.random.fold_in(keys[4], part), 71), part)
    face_couplings = bell_draw(own_keys[2], (3, ELEMS, NB, NB), 0.02, 0.119628906, ((1, 16),))
    face_order = jax.vmap(lambda own: jax.random.permutation(own, NB))(jax.random.split(keys[3], 3 * ELEMS)).reshape((3, ELEMS, NB)).astype(jnp.int32)
    return dict(orbitals=orbitals, element_blocks=element_blocks, face_couplings=face_couplings, face_order=face_order)


spectrum_top = 14.0
mean_epsilon = 1e-06

def build_coupled(face_couplings, face_order):
    columns = jnp.arange(face_order.shape[-1], dtype=jnp.int32)
    selector = (face_order[:, :, :, None] == columns[None, None, None, :]).astype(jnp.float32)
    return jnp.einsum('deri,deic->derc', face_couplings.astype(jnp.float32), selector).astype(jnp.bfloat16)

def apply_operator(blocks, coupled, values):
    wide = values.astype(jnp.float32)
    total = jnp.einsum('xyzij,xyzjc->xyzic', blocks.astype(jnp.float32), wide)
    for axis_number in range(3):
        faces = coupled[axis_number].astype(jnp.float32)
        before = jnp.roll(wide, 1, axis_number)
        after = jnp.roll(wide, -1, axis_number)
        faces_after = jnp.roll(faces, -1, axis_number)
        total = total + jnp.einsum('xyzij,xyzjc->xyzic', faces, before)
        total = total + jnp.einsum('xyzji,xyzjc->xyzic', faces_after, after)
    return total

def reference(orbitals, element_blocks, face_couplings, face_order):
    coupled = build_coupled(face_couplings, face_order).reshape(3, NXE, EY, EZ, NB, NB)
    blocks = element_blocks.reshape(NXE, EY, EZ, NB, NB)
    start_blocks = orbitals.reshape(NXE, EY, EZ, NB, NORB)
    product = apply_operator(blocks, coupled, start_blocks)
    start_values = start_blocks.astype(jnp.float32)
    total_count = float(ROWS * NORB)
    energy = jnp.sum(start_values * product)
    weight = jnp.sum(start_values * start_values)
    cut_level = energy / total_count / (weight / total_count + mean_epsilon)
    center = (spectrum_top + cut_level) * 0.5
    half_width = (spectrum_top - cut_level) * 0.5
    first_step = ((product - center * start_values) / half_width).astype(jnp.bfloat16)
    second_product = apply_operator(blocks, coupled, first_step)
    filtered = (2.0 * (second_product - center * first_step.astype(jnp.float32)) / half_width - start_values).astype(jnp.bfloat16)
    filtered = filtered.reshape(ROWS, NORB)
    gram_matrix = jnp.dot(filtered.T.astype(jnp.float32), filtered.astype(jnp.float32), preferred_element_type=jnp.float32) / float(ROWS)
    factor = jnp.linalg.cholesky(gram_matrix)
    solved = jax.scipy.linalg.solve_triangular(factor, filtered.astype(jnp.float32).T, lower=True)
    return solved.T.astype(jnp.bfloat16)
```

```python
import functools

import jax
import jax.numpy as jnp
from jax import lax
from jax.experimental import pallas as pl
from jax.experimental.pallas import tpu as pltpu
from jax.sharding import PartitionSpec as P

EY = 2
EZ = 2
BLOCK = 128


spectrum_top = 14.0
mean_epsilon = 1e-06


def from_behind(block, axis, distance):
    devices = range(lax.axis_size(axis))
    route = [((i - distance) % len(devices), i) for i in devices]
    return lax.ppermute(block, axis, route)


def extended(block, sides, width):
    for axis, dim in sides:
        count = lax.axis_size(axis)
        forward = [(i, i + 1) for i in range(count - 1)]
        forward.append((count - 1, 0))
        backward = [(target, source) for source, target in forward]
        low = lax.ppermute(
            lax.slice_in_dim(block, block.shape[dim] - width, None, axis=dim), axis, forward
        )
        high = lax.ppermute(lax.slice_in_dim(block, 0, width, axis=dim), axis, backward)
        block = jnp.concatenate([low, block, high], axis=dim)
    return block


def build_coupled(face_couplings, face_order):
    columns = jnp.arange(face_order.shape[-1], dtype=jnp.int32)
    selector = (face_order[:, :, :, None] == columns[None, None, None, :]).astype(jnp.bfloat16)
    return jnp.einsum(
        "deri,deic->derc", face_couplings, selector, preferred_element_type=jnp.float32
    ).astype(jnp.bfloat16)


def apply_blocks(blocks, coupled, next_faces, padded):
    centre = padded[1:-1]
    total = jnp.einsum("xyzij,xyzjc->xyzic", blocks, centre, preferred_element_type=jnp.float32)
    total = total + jnp.einsum(
        "xyzij,xyzjc->xyzic", coupled[0], padded[:-2], preferred_element_type=jnp.float32
    )
    total = total + jnp.einsum(
        "xyzji,xyzjc->xyzic", next_faces, padded[2:], preferred_element_type=jnp.float32
    )
    for axis_number in (1, 2):
        faces = coupled[axis_number]
        before = jnp.roll(centre, 1, axis_number)
        after = jnp.roll(centre, -1, axis_number)
        faces_after = jnp.roll(faces, -1, axis_number)
        total = total + jnp.einsum(
            "xyzij,xyzjc->xyzic", faces, before, preferred_element_type=jnp.float32
        )
        total = total + jnp.einsum(
            "xyzji,xyzjc->xyzic", faces_after, after, preferred_element_type=jnp.float32
        )
    return total


def filter_scalars(start_values, product, total_count):
    energy, weight = lax.psum(
        (jnp.sum(start_values * product), jnp.sum(start_values * start_values)), "ex"
    )
    cut_level = energy / total_count / (weight / total_count + mean_epsilon)
    return ((spectrum_top + cut_level) * 0.5, (spectrum_top - cut_level) * 0.5)


def dot_split(a, b, dims):
    a_high = a.astype(jnp.bfloat16)
    a_low = (a - a_high.astype(jnp.float32)).astype(jnp.bfloat16)
    b_high = b.astype(jnp.bfloat16)
    b_low = (b - b_high.astype(jnp.float32)).astype(jnp.bfloat16)

    def part(x, y):
        return lax.dot_general(x, y, (dims, ((), ())), preferred_element_type=jnp.float32)

    return part(a_high, b_high) + (part(a_high, b_low) + part(a_low, b_high))


def inverse_factor(block):
    tiles = BLOCK // 8
    lane = lax.broadcasted_iota(jnp.int32, (1, BLOCK), 1)
    sub = lax.broadcasted_iota(jnp.int32, (8, 1), 0)

    def group(step, state):
        state = list(state)
        for j in range(8):
            here = lane == j
            head = state[0]
            pivot = head[j : j + 1, j : j + 1]
            scale = lax.rsqrt(pivot)
            row = jnp.where(here, 1.0, head[j : j + 1, :])
            scaled = row * scale
            used = scaled * scale
            for t in range(tiles):
                column = state[t][:, j : j + 1]
                if t == 0:
                    column = jnp.where(sub > j, column, 0.0)
                    kept = jnp.where(here & (sub > j), 0.0, state[t])
                    new = kept - column * used
                    state[t] = jnp.where(sub == j, scaled, new)
                else:
                    live = t < tiles - step
                    new = jnp.where(here, 0.0, state[t]) - column * used
                    state[t] = jnp.where(live, new, state[t])
        state = [pltpu.roll(x, BLOCK - 8, 1) for x in state]
        return tuple(state[1:] + state[:1])

    state = tuple(block[8 * t : 8 * t + 8, :] for t in range(tiles))
    state = lax.fori_loop(0, tiles, group, state)
    full = jnp.concatenate(state, axis=0)
    rows = lax.broadcasted_iota(jnp.int32, (BLOCK, BLOCK), 0)
    columns = lax.broadcasted_iota(jnp.int32, (BLOCK, BLOCK), 1)
    return jnp.where(columns <= rows, full, 0.0)


def orthonormal_kernel(row_count, gram_ref, filtered_ref, out_ref, work):
    size = gram_ref.shape[0]
    work[...] = gram_ref[...] * (1.0 / row_count)
    for start in range(0, size, BLOCK):
        stop = start + BLOCK
        inverse = inverse_factor(work[start:stop, start:stop])
        if start > 0:
            work[start:stop, :start] = dot_split(inverse, work[start:stop, :start], ((1,), (0,)))
        work[start:stop, start:stop] = inverse
        if stop < size:
            upper = dot_split(inverse, work[start:stop, stop:], ((1,), (0,)))
            work[start:stop, stop:] = upper
            work[stop:, start:stop] = jnp.zeros((size - stop, BLOCK), jnp.float32)
            lower = upper.T
            for column in range(0, size, 256):
                work[stop:, column : column + 256] -= dot_split(
                    lower, work[start:stop, column : column + 256], ((1,), (0,))
                )
    for start in range(0, size, 256):
        stop = start + 256
        rows = lax.broadcasted_iota(jnp.int32, (256, stop), 0) + start
        columns = lax.broadcasted_iota(jnp.int32, (256, stop), 1)
        wide = jnp.where(columns <= rows, work[start:stop, :stop], 0.0)
        high = wide.astype(jnp.bfloat16)
        low = (wide - high.astype(jnp.float32)).astype(jnp.bfloat16)
        total = lax.dot_general(
            filtered_ref[:, :stop], high, (((1,), (1,)), ((), ())),
            preferred_element_type=jnp.float32,
        )
        total = total + lax.dot_general(
            filtered_ref[:, :stop], low, (((1,), (1,)), ((), ())),
            preferred_element_type=jnp.float32,
        )
        out_ref[:, start:stop] = total.astype(jnp.bfloat16)


def orthonormalize(summed_gram, filtered, row_count):
    whole = pl.BlockSpec(memory_space=pltpu.VMEM)
    return pl.pallas_call(
        functools.partial(orthonormal_kernel, float(row_count)),
        out_shape=jax.ShapeDtypeStruct(filtered.shape, jnp.bfloat16),
        in_specs=[whole, whole],
        out_specs=whole,
        scratch_shapes=[pltpu.VMEM(summed_gram.shape, jnp.float32)],
        compiler_params=pltpu.CompilerParams(vmem_limit_bytes=48 * 1024 * 1024),
    )(summed_gram, filtered)


def on_device(orbitals, element_blocks, face_couplings, face_order):
    local_rows, orbital_count = orbitals.shape
    elements = element_blocks.shape[0]
    basis_size = element_blocks.shape[1]
    layers = elements // (EY * EZ)
    slab_rows = EY * EZ * basis_size
    total_rows = local_rows * lax.axis_size("ex")
    total_count = float(total_rows * orbital_count)
    coupled = build_coupled(face_couplings, face_order).reshape(
        3, layers, EY, EZ, basis_size, basis_size
    )
    blocks = element_blocks.reshape(layers, EY, EZ, basis_size, basis_size)
    beyond = from_behind(coupled[0, 0], "ex", -1)
    next_faces = jnp.concatenate([coupled[0, 1:], beyond[None]], axis=0)
    start_blocks = orbitals.reshape(layers, EY, EZ, basis_size, orbital_count)
    start_values = start_blocks.astype(jnp.float32)

    def neighbour_product(values):
        flat_values = values.reshape(local_rows, orbital_count)
        padded = extended(flat_values, (("ex", 0),), slab_rows)
        padded = padded.reshape(layers + 2, EY, EZ, basis_size, orbital_count)
        return apply_blocks(blocks, coupled, next_faces, padded)

    product = neighbour_product(start_blocks)
    center, half_width = filter_scalars(start_values, product, total_count)
    first_step = ((product - center * start_values) / half_width).astype(jnp.bfloat16)
    second_product = neighbour_product(first_step)
    filtered = (
        2.0 * (second_product - center * first_step.astype(jnp.float32)) / half_width - start_values
    ).astype(jnp.bfloat16)
    filtered = filtered.reshape(local_rows, orbital_count)
    summed_gram = lax.psum(
        jnp.einsum("rc,rd->cd", filtered, filtered, preferred_element_type=jnp.float32), "ex"
    )
    return orthonormalize(summed_gram, filtered, total_rows)


def solution(mesh):
    in_specs = (
        P(("groups", "ex"), None),
        P(("groups", "ex"), None, None),
        P(None, ("groups", "ex"), None, None),
        P(None, "ex", None),
    )
    out_specs = P(("groups", "ex"), None)
    return jax.shard_map(
        on_device, mesh=mesh, in_specs=in_specs, out_specs=out_specs, check_vma=False
    )
```

```python
import functools

import jax
import jax.numpy as jnp
from jax import lax
from jax.experimental import pallas as pl
from jax.experimental.pallas import tpu as pltpu
from jax.sharding import PartitionSpec as P

EY = 2
EZ = 2
BLOCK = 128


spectrum_top = 14.0
mean_epsilon = 1e-06


def from_behind(block, axis, distance):
    devices = range(lax.axis_size(axis))
    route = [((i - distance) % len(devices), i) for i in devices]
    return lax.ppermute(block, axis, route)


def extended(block, sides, width):
    for axis, dim in sides:
        count = lax.axis_size(axis)
        forward = [(i, i + 1) for i in range(count - 1)]
        forward.append((count - 1, 0))
        backward = [(target, source) for source, target in forward]
        low = lax.ppermute(
            lax.slice_in_dim(block, block.shape[dim] - width, None, axis=dim), axis, forward
        )
        high = lax.ppermute(lax.slice_in_dim(block, 0, width, axis=dim), axis, backward)
        block = jnp.concatenate([low, block, high], axis=dim)
    return block


def build_coupled(face_couplings, face_order):
    columns = jnp.arange(face_order.shape[-1], dtype=jnp.int32)
    selector = (face_order[:, :, :, None] == columns[None, None, None, :]).astype(jnp.bfloat16)
    return jnp.einsum(
        "deri,deic->derc", face_couplings, selector, preferred_element_type=jnp.float32
    ).astype(jnp.bfloat16)


def apply_blocks(blocks, coupled, next_faces, padded):
    centre = padded[1:-1]
    total = jnp.einsum("xyzij,xyzjc->xyzic", blocks, centre, preferred_element_type=jnp.float32)
    total = total + jnp.einsum(
        "xyzij,xyzjc->xyzic", coupled[0], padded[:-2], preferred_element_type=jnp.float32
    )
    total = total + jnp.einsum(
        "xyzji,xyzjc->xyzic", next_faces, padded[2:], preferred_element_type=jnp.float32
    )
    for axis_number in (1, 2):
        faces = coupled[axis_number]
        before = jnp.roll(centre, 1, axis_number)
        after = jnp.roll(centre, -1, axis_number)
        faces_after = jnp.roll(faces, -1, axis_number)
        total = total + jnp.einsum(
            "xyzij,xyzjc->xyzic", faces, before, preferred_element_type=jnp.float32
        )
        total = total + jnp.einsum(
            "xyzji,xyzjc->xyzic", faces_after, after, preferred_element_type=jnp.float32
        )
    return total


def filter_scalars(start_values, product, total_count):
    energy, weight = sum_scalars(
        jnp.sum(start_values * product), jnp.sum(start_values * start_values)
    )
    cut_level = energy / total_count / (weight / total_count + mean_epsilon)
    return ((spectrum_top + cut_level) * 0.5, (spectrum_top - cut_level) * 0.5)


def dot_split(a, b, dims):
    a_high = a.astype(jnp.bfloat16)
    a_low = (a - a_high.astype(jnp.float32)).astype(jnp.bfloat16)
    b_high = b.astype(jnp.bfloat16)
    b_low = (b - b_high.astype(jnp.float32)).astype(jnp.bfloat16)

    def part(x, y):
        return lax.dot_general(x, y, (dims, ((), ())), preferred_element_type=jnp.float32)

    return part(a_high, b_high) + (part(a_high, b_low) + part(a_low, b_high))


def inverse_factor(block):
    tiles = BLOCK // 8
    lane = lax.broadcasted_iota(jnp.int32, (1, BLOCK), 1)
    sub = lax.broadcasted_iota(jnp.int32, (8, 1), 0)

    def group(step, state):
        state = list(state)
        for j in range(8):
            here = lane == j
            head = state[0]
            pivot = head[j : j + 1, j : j + 1]
            scale = lax.rsqrt(pivot)
            row = jnp.where(here, 1.0, head[j : j + 1, :])
            scaled = row * scale
            used = scaled * scale
            for t in range(tiles):
                column = state[t][:, j : j + 1]
                if t == 0:
                    column = jnp.where(sub > j, column, 0.0)
                    kept = jnp.where(here & (sub > j), 0.0, state[t])
                    new = kept - column * used
                    state[t] = jnp.where(sub == j, scaled, new)
                else:
                    live = t < tiles - step
                    new = jnp.where(here, 0.0, state[t]) - column * used
                    state[t] = jnp.where(live, new, state[t])
        state = [pltpu.roll(x, BLOCK - 8, 1) for x in state]
        return tuple(state[1:] + state[:1])

    state = tuple(block[8 * t : 8 * t + 8, :] for t in range(tiles))
    state = lax.fori_loop(0, tiles, group, state)
    full = jnp.concatenate(state, axis=0)
    rows = lax.broadcasted_iota(jnp.int32, (BLOCK, BLOCK), 0)
    columns = lax.broadcasted_iota(jnp.int32, (BLOCK, BLOCK), 1)
    return jnp.where(columns <= rows, full, 0.0)


def partner_of(me, bit):
    distance = 1 << bit
    side = lax.rem(lax.div(me, distance), 2)
    return me + distance * (1 - 2 * side), side


def greet(axis, bits):
    me = lax.axis_index(axis)
    barrier = pltpu.get_barrier_semaphore()
    for bit in bits:
        other, _ = partner_of(me, bit)
        pl.semaphore_signal(
            barrier, inc=1, device_id={axis: other}, device_id_type=pl.DeviceIdType.MESH
        )
    pl.semaphore_wait(barrier, len(bits))
    return me


def scalar_sum_kernel(bits, own_ref, out_ref, held, landed, send_sem, recv_sem):
    me = greet("ex", bits)
    held[0] = own_ref[...]
    for step, bit in enumerate(bits):
        other, _ = partner_of(me, bit)
        copy = pltpu.make_async_remote_copy(
            src_ref=held.at[step],
            dst_ref=landed.at[step],
            send_sem=send_sem.at[step],
            recv_sem=recv_sem.at[step],
            device_id={"ex": other},
            device_id_type=pl.DeviceIdType.MESH,
        )
        copy.start()
        copy.wait()
        held[step + 1] = held[step] + landed[step]
    out_ref[...] = held[len(bits)]


def bits_of(axis):
    count = lax.axis_size(axis)
    return list(range(count.bit_length() - 1))


def sum_scalars(first, second):
    bits = bits_of("ex")
    rows = lax.broadcasted_iota(jnp.int32, (8, 128), 0)
    own = jnp.where(rows < 4, first, second)
    whole = pl.BlockSpec(memory_space=pltpu.VMEM)
    total = pl.pallas_call(
        functools.partial(scalar_sum_kernel, bits),
        out_shape=jax.ShapeDtypeStruct((8, 128), jnp.float32),
        in_specs=[whole],
        out_specs=whole,
        scratch_shapes=[
            pltpu.VMEM((len(bits) + 1, 8, 128), jnp.float32),
            pltpu.VMEM((len(bits), 8, 128), jnp.float32),
            pltpu.SemaphoreType.DMA((len(bits),)),
            pltpu.SemaphoreType.DMA((len(bits),)),
        ],
        compiler_params=pltpu.CompilerParams(collective_id=0, has_side_effects=True),
    )(own)
    return total[0, 0], total[4, 0]


def gram_sum_kernel(streams, gram_ref, out_ref, work, landed, send_sem, recv_sem):
    me = greet("ex", sorted(streams[0][2]))
    blocks = gram_ref.shape[0] // BLOCK
    place = 0
    for i in range(blocks):
        for j in range(i + 1):
            tile = gram_ref[i * BLOCK : (i + 1) * BLOCK, j * BLOCK : (j + 1) * BLOCK]
            work[place : place + BLOCK // 8] = tile.reshape(BLOCK // 8, 8, 128)
            place += BLOCK // 8
    steps = len(streams[0][2])
    offsets = [start for start, _, _ in streams]
    lengths = [length for _, length, _ in streams]
    landings = [start for start, _, _ in streams]

    def send(s, source, target, number, other):
        copy = pltpu.make_async_remote_copy(
            src_ref=source,
            dst_ref=target,
            send_sem=send_sem.at[s, number],
            recv_sem=recv_sem.at[s, number],
            device_id={"ex": other},
            device_id_type=pl.DeviceIdType.MESH,
        )
        copy.start()
        return copy

    def scatter(s, step):
        other, side = partner_of(me, streams[s][2][step])
        half = lengths[s] // 2
        given = offsets[s] + (1 - side) * half
        lengths[s] = half
        offsets[s] = offsets[s] + side * half
        landing = landings[s]
        landings[s] = landing + half
        copy = send(s, work.at[pl.ds(given, half)], landed.at[pl.ds(landing, half)], step, other)
        return copy, landing

    def gather(s, step):
        bit = streams[s][2][steps - 1 - step]
        other, side = partner_of(me, bit)
        here = pl.ds(offsets[s], lengths[s])
        copy = send(s, out_ref.at[here], out_ref.at[here], steps + step, other)
        offsets[s] = offsets[s] - side * lengths[s]
        lengths[s] = lengths[s] * 2
        return copy

    several = range(len(streams))
    flying = [scatter(s, 0) for s in several]
    for step in range(steps):
        for s in several:
            copy, landing = flying[s]
            copy.wait()
            kept = pl.ds(offsets[s], lengths[s])
            total = work[kept] + landed[landing : landing + lengths[s]]
            if step + 1 < steps:
                work[kept] = total
                flying[s] = scatter(s, step + 1)
            else:
                out_ref[kept] = total
                flying[s] = gather(s, 0)
    for step in range(steps):
        for s in several:
            flying[s].wait()
            if step + 1 < steps:
                flying[s] = gather(s, step + 1)


def sum_gram(gram):
    bits = bits_of("ex")
    count = lax.axis_size("ex")
    blocks = gram.shape[0] // BLOCK
    tiles = blocks * (blocks + 1) // 2 * (BLOCK // 8)
    cut = tiles // count // 2 * count
    streams = [(0, cut, bits), (cut, tiles - cut, bits[:1] + bits[2:] + bits[1:2])]
    whole = pl.BlockSpec(memory_space=pltpu.VMEM)
    return pl.pallas_call(
        functools.partial(gram_sum_kernel, streams),
        out_shape=jax.ShapeDtypeStruct((tiles, 8, 128), jnp.float32),
        in_specs=[whole],
        out_specs=whole,
        scratch_shapes=[
            pltpu.VMEM((tiles, 8, 128), jnp.float32),
            pltpu.VMEM((tiles, 8, 128), jnp.float32),
            pltpu.SemaphoreType.DMA((2, 2 * len(bits))),
            pltpu.SemaphoreType.DMA((2, 2 * len(bits))),
        ],
        compiler_params=pltpu.CompilerParams(
            collective_id=1, has_side_effects=True, vmem_limit_bytes=32 * 1024 * 1024
        ),
    )(gram)


def orthonormal_kernel(row_count, gram_ref, filtered_ref, out_ref, work):
    size = work.shape[0]
    place = 0
    for i in range(size // BLOCK):
        for j in range(i + 1):
            tile = gram_ref[place : place + BLOCK // 8].reshape(BLOCK, BLOCK)
            work[i * BLOCK : (i + 1) * BLOCK, j * BLOCK : (j + 1) * BLOCK] = tile * (1.0 / row_count)
            place += BLOCK // 8
    for start in range(0, size, BLOCK):
        stop = start + BLOCK
        inverse = inverse_factor(work[start:stop, start:stop])
        if start > 0:
            work[start:stop, :start] = dot_split(inverse, work[start:stop, :start], ((1,), (0,)))
        work[start:stop, start:stop] = inverse
        if stop < size:
            lower = dot_split(work[stop:, start:stop], inverse, ((1,), (1,)))
            work[start:stop, stop:] = lower.T
            work[stop:, start:stop] = jnp.zeros((size - stop, BLOCK), jnp.float32)
            for column in range(0, size, BLOCK):
                first = max(stop, column)
                work[first:, column : column + BLOCK] -= dot_split(
                    lower[first - stop :], work[start:stop, column : column + BLOCK], ((1,), (0,))
                )
    for start in range(0, size, 256):
        stop = start + 256
        rows = lax.broadcasted_iota(jnp.int32, (256, stop), 0) + start
        columns = lax.broadcasted_iota(jnp.int32, (256, stop), 1)
        wide = jnp.where(columns <= rows, work[start:stop, :stop], 0.0)
        high = wide.astype(jnp.bfloat16)
        low = (wide - high.astype(jnp.float32)).astype(jnp.bfloat16)
        total = lax.dot_general(
            filtered_ref[:, :stop], high, (((1,), (1,)), ((), ())),
            preferred_element_type=jnp.float32,
        )
        total = total + lax.dot_general(
            filtered_ref[:, :stop], low, (((1,), (1,)), ((), ())),
            preferred_element_type=jnp.float32,
        )
        out_ref[:, start:stop] = total.astype(jnp.bfloat16)


def orthonormalize(summed_gram, filtered, row_count):
    whole = pl.BlockSpec(memory_space=pltpu.VMEM)
    return pl.pallas_call(
        functools.partial(orthonormal_kernel, float(row_count)),
        out_shape=jax.ShapeDtypeStruct(filtered.shape, jnp.bfloat16),
        in_specs=[whole, whole],
        out_specs=whole,
        scratch_shapes=[pltpu.VMEM((filtered.shape[1],) * 2, jnp.float32)],
        compiler_params=pltpu.CompilerParams(vmem_limit_bytes=48 * 1024 * 1024),
    )(summed_gram, filtered)


def on_device(orbitals, element_blocks, face_couplings, face_order):
    local_rows, orbital_count = orbitals.shape
    elements = element_blocks.shape[0]
    basis_size = element_blocks.shape[1]
    layers = elements // (EY * EZ)
    slab_rows = EY * EZ * basis_size
    total_rows = local_rows * lax.axis_size("ex")
    total_count = float(total_rows * orbital_count)
    coupled = build_coupled(face_couplings, face_order).reshape(
        3, layers, EY, EZ, basis_size, basis_size
    )
    blocks = element_blocks.reshape(layers, EY, EZ, basis_size, basis_size)
    beyond = from_behind(coupled[0, 0], "ex", -1)
    next_faces = jnp.concatenate([coupled[0, 1:], beyond[None]], axis=0)
    start_blocks = orbitals.reshape(layers, EY, EZ, basis_size, orbital_count)
    start_values = start_blocks.astype(jnp.float32)

    def neighbour_product(values):
        flat_values = values.reshape(local_rows, orbital_count)
        padded = extended(flat_values, (("ex", 0),), slab_rows)
        padded = padded.reshape(layers + 2, EY, EZ, basis_size, orbital_count)
        return apply_blocks(blocks, coupled, next_faces, padded)

    product = neighbour_product(start_blocks)
    center, half_width = filter_scalars(start_values, product, total_count)
    first_step = ((product - center * start_values) / half_width).astype(jnp.bfloat16)
    second_product = neighbour_product(first_step)
    filtered = (
        2.0 * (second_product - center * first_step.astype(jnp.float32)) / half_width - start_values
    ).astype(jnp.bfloat16)
    filtered = filtered.reshape(local_rows, orbital_count)
    summed_gram = sum_gram(
        jnp.einsum("rc,rd->cd", filtered, filtered, preferred_element_type=jnp.float32)
    )
    return orthonormalize(summed_gram, filtered, total_rows)


def solution(mesh):
    in_specs = (
        P(("groups", "ex"), None),
        P(("groups", "ex"), None, None),
        P(None, ("groups", "ex"), None, None),
        P(None, "ex", None),
    )
    out_specs = P(("groups", "ex"), None)
    return jax.shard_map(
        on_device, mesh=mesh, in_specs=in_specs, out_specs=out_specs, check_vma=False
    )
```

```python
import functools

import jax
import jax.numpy as jnp
from jax import lax
from jax.experimental import pallas as pl
from jax.experimental.pallas import tpu as pltpu
from jax.sharding import PartitionSpec as P

EY = 2
EZ = 2
BLOCK = 128


spectrum_top = 14.0
mean_epsilon = 1e-06


def from_behind(block, axis, distance):
    devices = range(lax.axis_size(axis))
    route = [((i - distance) % len(devices), i) for i in devices]
    return lax.ppermute(block, axis, route)


def extended(block, sides, width):
    for axis, dim in sides:
        count = lax.axis_size(axis)
        forward = [(i, i + 1) for i in range(count - 1)]
        forward.append((count - 1, 0))
        backward = [(target, source) for source, target in forward]
        low = lax.ppermute(
            lax.slice_in_dim(block, block.shape[dim] - width, None, axis=dim), axis, forward
        )
        high = lax.ppermute(lax.slice_in_dim(block, 0, width, axis=dim), axis, backward)
        block = jnp.concatenate([low, block, high], axis=dim)
    return block


def build_coupled(face_couplings, face_order):
    columns = jnp.arange(face_order.shape[-1], dtype=jnp.int32)
    selector = (face_order[:, :, :, None] == columns[None, None, None, :]).astype(jnp.bfloat16)
    return jnp.einsum(
        "deri,deic->derc", face_couplings, selector, preferred_element_type=jnp.float32
    ).astype(jnp.bfloat16)


def apply_blocks(blocks, coupled, next_faces, padded):
    centre = padded[1:-1]
    total = jnp.einsum("xyzij,xyzjc->xyzic", blocks, centre, preferred_element_type=jnp.float32)
    total = total + jnp.einsum(
        "xyzij,xyzjc->xyzic", coupled[0], padded[:-2], preferred_element_type=jnp.float32
    )
    total = total + jnp.einsum(
        "xyzji,xyzjc->xyzic", next_faces, padded[2:], preferred_element_type=jnp.float32
    )
    for axis_number in (1, 2):
        faces = coupled[axis_number]
        before = jnp.roll(centre, 1, axis_number)
        after = jnp.roll(centre, -1, axis_number)
        faces_after = jnp.roll(faces, -1, axis_number)
        total = total + jnp.einsum(
            "xyzij,xyzjc->xyzic", faces, before, preferred_element_type=jnp.float32
        )
        total = total + jnp.einsum(
            "xyzji,xyzjc->xyzic", faces_after, after, preferred_element_type=jnp.float32
        )
    return total


def filter_scalars(start_values, product, total_count):
    energy, weight = sum_scalars(
        jnp.sum(start_values * product), jnp.sum(start_values * start_values)
    )
    cut_level = energy / total_count / (weight / total_count + mean_epsilon)
    return ((spectrum_top + cut_level) * 0.5, (spectrum_top - cut_level) * 0.5)


def dot_split(a, b, dims):
    a_high = a.astype(jnp.bfloat16)
    a_low = (a - a_high.astype(jnp.float32)).astype(jnp.bfloat16)
    b_high = b.astype(jnp.bfloat16)
    b_low = (b - b_high.astype(jnp.float32)).astype(jnp.bfloat16)

    def part(x, y):
        return lax.dot_general(x, y, (dims, ((), ())), preferred_element_type=jnp.float32)

    return part(a_high, b_high) + (part(a_high, b_low) + part(a_low, b_high))


def inverse_factor(block):
    tiles = BLOCK // 8
    lane = lax.broadcasted_iota(jnp.int32, (1, BLOCK), 1)
    sub = lax.broadcasted_iota(jnp.int32, (8, 1), 0)

    def group(step, state):
        head = state[0]
        columns = [jnp.broadcast_to(head[:, j : j + 1], (8, BLOCK)) for j in range(8)]
        rows = jnp.where(lane < 8, jnp.where(lane == sub, 1.0, 0.0), head)
        for j in range(8):
            factor = jnp.where(sub > j, columns[j] * (1.0 / columns[j][j : j + 1, :]), 0.0)
            for k in range(j + 1, 8):
                columns[k] = columns[k] - factor * columns[k][j : j + 1, :]
            rows = rows - factor * rows[j : j + 1, :]
        pivots = columns[0]
        for j in range(1, 8):
            pivots = jnp.where(sub == j, columns[j], pivots)
        inverse = 1.0 / pivots
        solved = rows * inverse
        for j in range(7, 0, -1):
            factor = jnp.where(sub < j, columns[j] * inverse, 0.0)
            solved = solved - factor * solved[j : j + 1, :]
        result = []
        for t in range(1, tiles):
            new = jnp.where(lane < 8, 0.0, state[t])
            for j in range(8):
                new = new - state[t][:, j : j + 1] * solved[j : j + 1, :]
            result.append(jnp.where(t < tiles - step, new, state[t]))
        result.append(rows * lax.rsqrt(pivots))
        return tuple(pltpu.roll(x, BLOCK - 8, 1) for x in result)

    state = tuple(block[8 * t : 8 * t + 8, :] for t in range(tiles))
    state = lax.fori_loop(0, tiles, group, state)
    full = jnp.concatenate(state, axis=0)
    rows = lax.broadcasted_iota(jnp.int32, (BLOCK, BLOCK), 0)
    columns = lax.broadcasted_iota(jnp.int32, (BLOCK, BLOCK), 1)
    return jnp.where(columns <= rows, full, 0.0)


def partner_of(me, bit):
    distance = 1 << bit
    side = lax.rem(lax.div(me, distance), 2)
    return me + distance * (1 - 2 * side), side


def greet(axis, bits):
    me = lax.axis_index(axis)
    barrier = pltpu.get_barrier_semaphore()
    for bit in bits:
        other, _ = partner_of(me, bit)
        pl.semaphore_signal(
            barrier, inc=1, device_id={axis: other}, device_id_type=pl.DeviceIdType.MESH
        )
    pl.semaphore_wait(barrier, len(bits))
    return me


def scalar_sum_kernel(bits, own_ref, out_ref, held, landed, send_sem, recv_sem):
    me = greet("ex", bits)
    held[0] = own_ref[...]
    for step, bit in enumerate(bits):
        other, _ = partner_of(me, bit)
        copy = pltpu.make_async_remote_copy(
            src_ref=held.at[step],
            dst_ref=landed.at[step],
            send_sem=send_sem.at[step],
            recv_sem=recv_sem.at[step],
            device_id={"ex": other},
            device_id_type=pl.DeviceIdType.MESH,
        )
        copy.start()
        copy.wait()
        held[step + 1] = held[step] + landed[step]
    out_ref[...] = held[len(bits)]


def bits_of(axis):
    count = lax.axis_size(axis)
    return list(range(count.bit_length() - 1))


def sum_scalars(first, second):
    bits = bits_of("ex")
    rows = lax.broadcasted_iota(jnp.int32, (8, 128), 0)
    own = jnp.where(rows < 4, first, second)
    whole = pl.BlockSpec(memory_space=pltpu.VMEM)
    total = pl.pallas_call(
        functools.partial(scalar_sum_kernel, bits),
        out_shape=jax.ShapeDtypeStruct((8, 128), jnp.float32),
        in_specs=[whole],
        out_specs=whole,
        scratch_shapes=[
            pltpu.VMEM((len(bits) + 1, 8, 128), jnp.float32),
            pltpu.VMEM((len(bits), 8, 128), jnp.float32),
            pltpu.SemaphoreType.DMA((len(bits),)),
            pltpu.SemaphoreType.DMA((len(bits),)),
        ],
        compiler_params=pltpu.CompilerParams(collective_id=0, has_side_effects=True),
    )(own)
    return total[0, 0], total[4, 0]


def gram_sum_kernel(streams, gram_ref, out_ref, work, landed, send_sem, recv_sem):
    me = greet("ex", sorted(streams[0][2]))
    blocks = gram_ref.shape[0] // BLOCK
    place = 0
    for i in range(blocks):
        for j in range(i + 1):
            tile = gram_ref[i * BLOCK : (i + 1) * BLOCK, j * BLOCK : (j + 1) * BLOCK]
            work[place : place + BLOCK // 8] = tile.reshape(BLOCK // 8, 8, 128)
            place += BLOCK // 8
    steps = len(streams[0][2])
    offsets = [start for start, _, _ in streams]
    lengths = [length for _, length, _ in streams]
    landings = [start for start, _, _ in streams]

    def send(s, source, target, number, other):
        copy = pltpu.make_async_remote_copy(
            src_ref=source,
            dst_ref=target,
            send_sem=send_sem.at[s, number],
            recv_sem=recv_sem.at[s, number],
            device_id={"ex": other},
            device_id_type=pl.DeviceIdType.MESH,
        )
        copy.start()
        return copy

    def scatter(s, step):
        other, side = partner_of(me, streams[s][2][step])
        half = lengths[s] // 2
        given = offsets[s] + (1 - side) * half
        lengths[s] = half
        offsets[s] = offsets[s] + side * half
        landing = landings[s]
        landings[s] = landing + half
        copy = send(s, work.at[pl.ds(given, half)], landed.at[pl.ds(landing, half)], step, other)
        return copy, landing

    def gather(s, step):
        bit = streams[s][2][steps - 1 - step]
        other, side = partner_of(me, bit)
        here = pl.ds(offsets[s], lengths[s])
        copy = send(s, out_ref.at[here], out_ref.at[here], steps + step, other)
        offsets[s] = offsets[s] - side * lengths[s]
        lengths[s] = lengths[s] * 2
        return copy

    several = range(len(streams))
    flying = [scatter(s, 0) for s in several]
    for step in range(steps):
        for s in several:
            copy, landing = flying[s]
            copy.wait()
            kept = pl.ds(offsets[s], lengths[s])
            total = work[kept] + landed[landing : landing + lengths[s]]
            if step + 1 < steps:
                work[kept] = total
                flying[s] = scatter(s, step + 1)
            else:
                out_ref[kept] = total
                flying[s] = gather(s, 0)
    for step in range(steps):
        for s in several:
            flying[s].wait()
            if step + 1 < steps:
                flying[s] = gather(s, step + 1)


def sum_gram(gram):
    bits = bits_of("ex")
    count = lax.axis_size("ex")
    blocks = gram.shape[0] // BLOCK
    tiles = blocks * (blocks + 1) // 2 * (BLOCK // 8)
    cut = tiles // count // 2 * count
    streams = [(0, cut, bits), (cut, tiles - cut, bits[:1] + bits[2:] + bits[1:2])]
    whole = pl.BlockSpec(memory_space=pltpu.VMEM)
    return pl.pallas_call(
        functools.partial(gram_sum_kernel, streams),
        out_shape=jax.ShapeDtypeStruct((tiles, 8, 128), jnp.float32),
        in_specs=[whole],
        out_specs=whole,
        scratch_shapes=[
            pltpu.VMEM((tiles, 8, 128), jnp.float32),
            pltpu.VMEM((tiles, 8, 128), jnp.float32),
            pltpu.SemaphoreType.DMA((2, 2 * len(bits))),
            pltpu.SemaphoreType.DMA((2, 2 * len(bits))),
        ],
        compiler_params=pltpu.CompilerParams(
            collective_id=1, has_side_effects=True, vmem_limit_bytes=32 * 1024 * 1024
        ),
    )(gram)


def orthonormal_kernel(row_count, gram_ref, filtered_ref, out_ref, work):
    size = work.shape[0]
    place = 0
    for i in range(size // BLOCK):
        for j in range(i + 1):
            tile = gram_ref[place : place + BLOCK // 8].reshape(BLOCK, BLOCK)
            work[i * BLOCK : (i + 1) * BLOCK, j * BLOCK : (j + 1) * BLOCK] = tile * (1.0 / row_count)
            place += BLOCK // 8
    for start in range(0, size, BLOCK):
        stop = start + BLOCK
        inverse = inverse_factor(work[start:stop, start:stop])
        if start > 0:
            work[start:stop, :start] = dot_split(inverse, work[start:stop, :start], ((1,), (0,)))
        work[start:stop, start:stop] = inverse
        if stop < size:
            lower = dot_split(work[stop:, start:stop], inverse, ((1,), (1,)))
            work[start:stop, stop:] = lower.T
            work[stop:, start:stop] = jnp.zeros((size - stop, BLOCK), jnp.float32)
            for column in range(0, size, BLOCK):
                first = max(stop, column)
                work[first:, column : column + BLOCK] -= dot_split(
                    lower[first - stop :], work[start:stop, column : column + BLOCK], ((1,), (0,))
                )
    for start in range(0, size, 256):
        stop = start + 256
        rows = lax.broadcasted_iota(jnp.int32, (256, stop), 0) + start
        columns = lax.broadcasted_iota(jnp.int32, (256, stop), 1)
        wide = jnp.where(columns <= rows, work[start:stop, :stop], 0.0)
        high = wide.astype(jnp.bfloat16)
        low = (wide - high.astype(jnp.float32)).astype(jnp.bfloat16)
        total = lax.dot_general(
            filtered_ref[:, :stop], high, (((1,), (1,)), ((), ())),
            preferred_element_type=jnp.float32,
        )
        total = total + lax.dot_general(
            filtered_ref[:, :stop], low, (((1,), (1,)), ((), ())),
            preferred_element_type=jnp.float32,
        )
        out_ref[:, start:stop] = total.astype(jnp.bfloat16)


def orthonormalize(summed_gram, filtered, row_count):
    whole = pl.BlockSpec(memory_space=pltpu.VMEM)
    return pl.pallas_call(
        functools.partial(orthonormal_kernel, float(row_count)),
        out_shape=jax.ShapeDtypeStruct(filtered.shape, jnp.bfloat16),
        in_specs=[whole, whole],
        out_specs=whole,
        scratch_shapes=[pltpu.VMEM((filtered.shape[1],) * 2, jnp.float32)],
        compiler_params=pltpu.CompilerParams(vmem_limit_bytes=48 * 1024 * 1024),
    )(summed_gram, filtered)


def on_device(orbitals, element_blocks, face_couplings, face_order):
    local_rows, orbital_count = orbitals.shape
    elements = element_blocks.shape[0]
    basis_size = element_blocks.shape[1]
    layers = elements // (EY * EZ)
    slab_rows = EY * EZ * basis_size
    total_rows = local_rows * lax.axis_size("ex")
    total_count = float(total_rows * orbital_count)
    coupled = build_coupled(face_couplings, face_order).reshape(
        3, layers, EY, EZ, basis_size, basis_size
    )
    blocks = element_blocks.reshape(layers, EY, EZ, basis_size, basis_size)
    beyond = from_behind(coupled[0, 0], "ex", -1)
    next_faces = jnp.concatenate([coupled[0, 1:], beyond[None]], axis=0)
    start_blocks = orbitals.reshape(layers, EY, EZ, basis_size, orbital_count)
    start_values = start_blocks.astype(jnp.float32)

    def neighbour_product(values):
        flat_values = values.reshape(local_rows, orbital_count)
        padded = extended(flat_values, (("ex", 0),), slab_rows)
        padded = padded.reshape(layers + 2, EY, EZ, basis_size, orbital_count)
        return apply_blocks(blocks, coupled, next_faces, padded)

    product = neighbour_product(start_blocks)
    center, half_width = filter_scalars(start_values, product, total_count)
    first_step = ((product - center * start_values) / half_width).astype(jnp.bfloat16)
    second_product = neighbour_product(first_step)
    filtered = (
        2.0 * (second_product - center * first_step.astype(jnp.float32)) / half_width - start_values
    ).astype(jnp.bfloat16)
    filtered = filtered.reshape(local_rows, orbital_count)
    summed_gram = sum_gram(
        jnp.einsum("rc,rd->cd", filtered, filtered, preferred_element_type=jnp.float32)
    )
    return orthonormalize(summed_gram, filtered, total_rows)


def solution(mesh):
    in_specs = (
        P(("groups", "ex"), None),
        P(("groups", "ex"), None, None),
        P(None, ("groups", "ex"), None, None),
        P(None, "ex", None),
    )
    out_specs = P(("groups", "ex"), None)
    return jax.shard_map(
        on_device, mesh=mesh, in_specs=in_specs, out_specs=out_specs, check_vma=False
    )
```

```python
import functools

import jax
import jax.numpy as jnp
from jax import lax
from jax.experimental import pallas as pl
from jax.experimental.pallas import tpu as pltpu
from jax.sharding import PartitionSpec as P

EY = 2
EZ = 2
BLOCK = 128
CHUNKS = 2


spectrum_top = 14.0
mean_epsilon = 1e-06


def from_behind(block, axis, distance):
    devices = range(lax.axis_size(axis))
    route = [((i - distance) % len(devices), i) for i in devices]
    return lax.ppermute(block, axis, route)


def halo(block, width):
    count = lax.axis_size("ex")
    forward = [(i, (i + 1) % count) for i in range(count)]
    backward = [(target, source) for source, target in forward]
    low = lax.ppermute(block[block.shape[0] - width :], "ex", forward)
    high = lax.ppermute(block[:width], "ex", backward)
    return low, high


def build_coupled(face_couplings, face_order):
    columns = jnp.arange(face_order.shape[-1], dtype=jnp.int32)
    selector = (face_order[:, :, :, None] == columns[None, None, None, :]).astype(jnp.bfloat16)
    return jnp.einsum(
        "deri,deic->derc", face_couplings, selector, preferred_element_type=jnp.float32
    ).astype(jnp.bfloat16)


def apply_blocks(blocks, coupled, next_faces, padded):
    centre = padded[1:-1]
    total = jnp.einsum("xyzij,xyzjc->xyzic", blocks, centre, preferred_element_type=jnp.float32)
    total = total + jnp.einsum(
        "xyzij,xyzjc->xyzic", coupled[0], padded[:-2], preferred_element_type=jnp.float32
    )
    total = total + jnp.einsum(
        "xyzji,xyzjc->xyzic", next_faces, padded[2:], preferred_element_type=jnp.float32
    )
    for axis_number in (1, 2):
        faces = coupled[axis_number]
        before = jnp.roll(centre, 1, axis_number)
        after = jnp.roll(centre, -1, axis_number)
        faces_after = jnp.roll(faces, -1, axis_number)
        total = total + jnp.einsum(
            "xyzij,xyzjc->xyzic", faces, before, preferred_element_type=jnp.float32
        )
        total = total + jnp.einsum(
            "xyzji,xyzjc->xyzic", faces_after, after, preferred_element_type=jnp.float32
        )
    return total


def filter_scalars(energy, weight, total_count):
    energy, weight = sum_scalars(energy, weight)
    cut_level = energy / total_count / (weight / total_count + mean_epsilon)
    return ((spectrum_top + cut_level) * 0.5, (spectrum_top - cut_level) * 0.5)


def dot_split(a, b, dims):
    a_high = a.astype(jnp.bfloat16)
    a_low = (a - a_high.astype(jnp.float32)).astype(jnp.bfloat16)
    b_high = b.astype(jnp.bfloat16)
    b_low = (b - b_high.astype(jnp.float32)).astype(jnp.bfloat16)

    def part(x, y):
        return lax.dot_general(x, y, (dims, ((), ())), preferred_element_type=jnp.float32)

    return part(a_high, b_high) + (part(a_high, b_low) + part(a_low, b_high))


def inverse_factor(block):
    tiles = BLOCK // 8
    lane = lax.broadcasted_iota(jnp.int32, (1, BLOCK), 1)
    sub = lax.broadcasted_iota(jnp.int32, (8, 1), 0)

    def group(step, state):
        head = state[0]
        columns = [jnp.broadcast_to(head[:, j : j + 1], (8, BLOCK)) for j in range(8)]
        rows = jnp.where(lane < 8, jnp.where(lane == sub, 1.0, 0.0), head)
        for j in range(8):
            factor = jnp.where(sub > j, columns[j] * (1.0 / columns[j][j : j + 1, :]), 0.0)
            for k in range(j + 1, 8):
                columns[k] = columns[k] - factor * columns[k][j : j + 1, :]
            rows = rows - factor * rows[j : j + 1, :]
        pivots = columns[0]
        for j in range(1, 8):
            pivots = jnp.where(sub == j, columns[j], pivots)
        inverse = 1.0 / pivots
        solved = rows * inverse
        for j in range(7, 0, -1):
            factor = jnp.where(sub < j, columns[j] * inverse, 0.0)
            solved = solved - factor * solved[j : j + 1, :]
        result = []
        for t in range(1, tiles):
            new = jnp.where(lane < 8, 0.0, state[t])
            for j in range(8):
                new = new - state[t][:, j : j + 1] * solved[j : j + 1, :]
            result.append(jnp.where(t < tiles - step, new, state[t]))
        result.append(rows * lax.rsqrt(pivots))
        return tuple(pltpu.roll(x, BLOCK - 8, 1) for x in result)

    state = tuple(block[8 * t : 8 * t + 8, :] for t in range(tiles))
    state = lax.fori_loop(0, tiles, group, state)
    full = jnp.concatenate(state, axis=0)
    rows = lax.broadcasted_iota(jnp.int32, (BLOCK, BLOCK), 0)
    columns = lax.broadcasted_iota(jnp.int32, (BLOCK, BLOCK), 1)
    return jnp.where(columns <= rows, full, 0.0)


def partner_of(me, bit):
    distance = 1 << bit
    side = lax.rem(lax.div(me, distance), 2)
    return me + distance * (1 - 2 * side), side


def greet(axis, bits):
    me = lax.axis_index(axis)
    barrier = pltpu.get_barrier_semaphore()
    for bit in bits:
        other, _ = partner_of(me, bit)
        pl.semaphore_signal(
            barrier, inc=1, device_id={axis: other}, device_id_type=pl.DeviceIdType.MESH
        )
    pl.semaphore_wait(barrier, len(bits))
    return me


def scalar_sum_kernel(bits, own_ref, out_ref, held, landed, send_sem, recv_sem):
    me = greet("ex", bits)
    held[0] = own_ref[...]
    for step, bit in enumerate(bits):
        other, _ = partner_of(me, bit)
        copy = pltpu.make_async_remote_copy(
            src_ref=held.at[step],
            dst_ref=landed.at[step],
            send_sem=send_sem.at[step],
            recv_sem=recv_sem.at[step],
            device_id={"ex": other},
            device_id_type=pl.DeviceIdType.MESH,
        )
        copy.start()
        copy.wait()
        held[step + 1] = held[step] + landed[step]
    out_ref[...] = held[len(bits)]


def bits_of(axis):
    count = lax.axis_size(axis)
    return list(range(count.bit_length() - 1))


def sum_scalars(first, second):
    bits = bits_of("ex")
    rows = lax.broadcasted_iota(jnp.int32, (8, 128), 0)
    own = jnp.where(rows < 4, first, second)
    whole = pl.BlockSpec(memory_space=pltpu.VMEM)
    total = pl.pallas_call(
        functools.partial(scalar_sum_kernel, bits),
        out_shape=jax.ShapeDtypeStruct((8, 128), jnp.float32),
        in_specs=[whole],
        out_specs=whole,
        scratch_shapes=[
            pltpu.VMEM((len(bits) + 1, 8, 128), jnp.float32),
            pltpu.VMEM((len(bits), 8, 128), jnp.float32),
            pltpu.SemaphoreType.DMA((len(bits),)),
            pltpu.SemaphoreType.DMA((len(bits),)),
        ],
        compiler_params=pltpu.CompilerParams(collective_id=0, has_side_effects=True),
    )(own)
    return total[0, 0], total[4, 0]


def gram_sum_kernel(streams, gram_ref, out_ref, work, landed, send_sem, recv_sem):
    me = greet("ex", sorted(streams[0][2]))
    blocks = gram_ref.shape[0] // BLOCK
    place = 0
    for i in range(blocks):
        for j in range(i + 1):
            tile = gram_ref[i * BLOCK : (i + 1) * BLOCK, j * BLOCK : (j + 1) * BLOCK]
            work[place : place + BLOCK // 8] = tile.reshape(BLOCK // 8, 8, 128)
            place += BLOCK // 8
    steps = len(streams[0][2])
    offsets = [start for start, _, _ in streams]
    lengths = [length for _, length, _ in streams]
    landings = [start for start, _, _ in streams]

    def send(s, source, target, number, other):
        copy = pltpu.make_async_remote_copy(
            src_ref=source,
            dst_ref=target,
            send_sem=send_sem.at[s, number],
            recv_sem=recv_sem.at[s, number],
            device_id={"ex": other},
            device_id_type=pl.DeviceIdType.MESH,
        )
        copy.start()
        return copy

    def scatter(s, step):
        other, side = partner_of(me, streams[s][2][step])
        half = lengths[s] // 2
        given = offsets[s] + (1 - side) * half
        lengths[s] = half
        offsets[s] = offsets[s] + side * half
        landing = landings[s]
        landings[s] = landing + half
        copy = send(s, work.at[pl.ds(given, half)], landed.at[pl.ds(landing, half)], step, other)
        return copy, landing

    def gather(s, step):
        bit = streams[s][2][steps - 1 - step]
        other, side = partner_of(me, bit)
        here = pl.ds(offsets[s], lengths[s])
        copy = send(s, out_ref.at[here], out_ref.at[here], steps + step, other)
        offsets[s] = offsets[s] - side * lengths[s]
        lengths[s] = lengths[s] * 2
        return copy

    several = range(len(streams))
    flying = [scatter(s, 0) for s in several]
    for step in range(steps):
        for s in several:
            copy, landing = flying[s]
            copy.wait()
            kept = pl.ds(offsets[s], lengths[s])
            total = work[kept] + landed[landing : landing + lengths[s]]
            if step + 1 < steps:
                work[kept] = total
                flying[s] = scatter(s, step + 1)
            else:
                out_ref[kept] = total
                flying[s] = gather(s, 0)
    for step in range(steps):
        for s in several:
            flying[s].wait()
            if step + 1 < steps:
                flying[s] = gather(s, step + 1)


def sum_gram(gram):
    bits = bits_of("ex")
    count = lax.axis_size("ex")
    blocks = gram.shape[0] // BLOCK
    tiles = blocks * (blocks + 1) // 2 * (BLOCK // 8)
    cut = tiles // count // 2 * count
    streams = [(0, cut, bits), (cut, tiles - cut, bits[:1] + bits[2:] + bits[1:2])]
    whole = pl.BlockSpec(memory_space=pltpu.VMEM)
    return pl.pallas_call(
        functools.partial(gram_sum_kernel, streams),
        out_shape=jax.ShapeDtypeStruct((tiles, 8, 128), jnp.float32),
        in_specs=[whole],
        out_specs=whole,
        scratch_shapes=[
            pltpu.VMEM((tiles, 8, 128), jnp.float32),
            pltpu.VMEM((tiles, 8, 128), jnp.float32),
            pltpu.SemaphoreType.DMA((2, 2 * len(bits))),
            pltpu.SemaphoreType.DMA((2, 2 * len(bits))),
        ],
        compiler_params=pltpu.CompilerParams(
            collective_id=1, has_side_effects=True, vmem_limit_bytes=32 * 1024 * 1024
        ),
    )(gram)


def orthonormal_kernel(row_count, gram_ref, filtered_ref, out_ref, work):
    size = work.shape[0]
    place = 0
    for i in range(size // BLOCK):
        for j in range(i + 1):
            tile = gram_ref[place : place + BLOCK // 8].reshape(BLOCK, BLOCK)
            work[i * BLOCK : (i + 1) * BLOCK, j * BLOCK : (j + 1) * BLOCK] = tile * (1.0 / row_count)
            place += BLOCK // 8
    for start in range(0, size, BLOCK):
        stop = start + BLOCK
        inverse = inverse_factor(work[start:stop, start:stop])
        if start > 0:
            work[start:stop, :start] = dot_split(inverse, work[start:stop, :start], ((1,), (0,)))
        work[start:stop, start:stop] = inverse
        if stop < size:
            lower = dot_split(work[stop:, start:stop], inverse, ((1,), (1,)))
            work[start:stop, stop:] = lower.T
            work[stop:, start:stop] = jnp.zeros((size - stop, BLOCK), jnp.float32)
            for column in range(0, size, BLOCK):
                first = max(stop, column)
                work[first:, column : column + BLOCK] -= dot_split(
                    lower[first - stop :], work[start:stop, column : column + BLOCK], ((1,), (0,))
                )
    for start in range(0, size, 256):
        stop = start + 256
        rows = lax.broadcasted_iota(jnp.int32, (256, stop), 0) + start
        columns = lax.broadcasted_iota(jnp.int32, (256, stop), 1)
        wide = jnp.where(columns <= rows, work[start:stop, :stop], 0.0)
        high = wide.astype(jnp.bfloat16)
        low = (wide - high.astype(jnp.float32)).astype(jnp.bfloat16)
        total = lax.dot_general(
            filtered_ref[:, :stop], high, (((1,), (1,)), ((), ())),
            preferred_element_type=jnp.float32,
        )
        total = total + lax.dot_general(
            filtered_ref[:, :stop], low, (((1,), (1,)), ((), ())),
            preferred_element_type=jnp.float32,
        )
        out_ref[:, start:stop] = total.astype(jnp.bfloat16)


def orthonormalize(summed_gram, filtered, row_count):
    whole = pl.BlockSpec(memory_space=pltpu.VMEM)
    return pl.pallas_call(
        functools.partial(orthonormal_kernel, float(row_count)),
        out_shape=jax.ShapeDtypeStruct(filtered.shape, jnp.bfloat16),
        in_specs=[whole, whole],
        out_specs=whole,
        scratch_shapes=[pltpu.VMEM((filtered.shape[1],) * 2, jnp.float32)],
        compiler_params=pltpu.CompilerParams(vmem_limit_bytes=48 * 1024 * 1024),
    )(summed_gram, filtered)


def on_device(orbitals, element_blocks, face_couplings, face_order):
    local_rows, orbital_count = orbitals.shape
    elements = element_blocks.shape[0]
    basis_size = element_blocks.shape[1]
    layers = elements // (EY * EZ)
    slab_rows = EY * EZ * basis_size
    total_rows = local_rows * lax.axis_size("ex")
    total_count = float(total_rows * orbital_count)
    coupled = build_coupled(face_couplings, face_order).reshape(
        3, layers, EY, EZ, basis_size, basis_size
    )
    blocks = element_blocks.reshape(layers, EY, EZ, basis_size, basis_size)
    beyond = from_behind(coupled[0, 0], "ex", -1)
    next_faces = jnp.concatenate([coupled[0, 1:], beyond[None]], axis=0)
    chunk = orbital_count // CHUNKS

    def neighbour_product(values, sides):
        padded = jnp.concatenate([sides[0], values, sides[1]], axis=0)
        padded = padded.reshape(layers + 2, EY, EZ, basis_size, chunk)
        return apply_blocks(blocks, coupled, next_faces, padded).reshape(local_rows, chunk)

    starts = [orbitals[:, i * chunk : (i + 1) * chunk] for i in range(CHUNKS)]
    sides = [halo(starts[0], slab_rows)]
    for i in range(1, CHUNKS):
        sent, sides[i - 1] = lax.optimization_barrier((starts[i], sides[i - 1]))
        sides.append(halo(sent, slab_rows))
    products = [neighbour_product(*pair) for pair in zip(starts, sides)]
    energy = sum(jnp.sum(v.astype(jnp.float32) * p) for v, p in zip(starts, products))
    weight = jnp.sum(jnp.square(orbitals.astype(jnp.float32)))
    rounded = [p.astype(jnp.bfloat16) for p in products]
    before = sides[CHUNKS - 1]
    second_sides = []
    for i in range(CHUNKS):
        if i > 0:
            sent, before = lax.optimization_barrier((rounded[i], before))
            second_sides[i - 1] = before
        else:
            sent = rounded[i]
        before = halo(sent, slab_rows)
        second_sides.append(before)
    energy, weight, second_sides[0] = lax.optimization_barrier((energy, weight, second_sides[0]))
    center, half_width = filter_scalars(energy, weight, total_count)
    parts = []
    for value, product, narrow, beside in zip(starts, products, rounded, second_sides):
        wide = value.astype(jnp.float32)
        twice = neighbour_product(narrow, beside)
        second = (twice - center * narrow.astype(jnp.float32)) / half_width
        first = (product - center * wide) / half_width
        parts.append((2.0 * (second - center * first) / half_width - wide).astype(jnp.bfloat16))
    filtered = jnp.concatenate(parts, axis=1)
    summed_gram = sum_gram(
        jnp.einsum("rc,rd->cd", filtered, filtered, preferred_element_type=jnp.float32)
    )
    return orthonormalize(summed_gram, filtered, total_rows)


def solution(mesh):
    in_specs = (
        P(("groups", "ex"), None),
        P(("groups", "ex"), None, None),
        P(None, ("groups", "ex"), None, None),
        P(None, "ex", None),
    )
    out_specs = P(("groups", "ex"), None)
    return jax.shard_map(
        on_device, mesh=mesh, in_specs=in_specs, out_specs=out_specs, check_vma=False
    )
```

```python
import functools

import jax
import jax.numpy as jnp
from jax import lax
from jax.experimental import pallas as pl
from jax.experimental.pallas import tpu as pltpu
from jax.sharding import PartitionSpec as P

EY = 2
EZ = 2
BLOCK = 128
CHUNKS = 2


spectrum_top = 14.0
mean_epsilon = 1e-06


def from_behind(block, axis, distance):
    devices = range(lax.axis_size(axis))
    route = [((i - distance) % len(devices), i) for i in devices]
    return lax.ppermute(block, axis, route)


def halo(block, width):
    count = lax.axis_size("ex")
    forward = [(i, (i + 1) % count) for i in range(count)]
    backward = [(target, source) for source, target in forward]
    low = lax.ppermute(block[block.shape[0] - width :], "ex", forward)
    high = lax.ppermute(block[:width], "ex", backward)
    return low, high


def build_coupled(face_couplings, face_order):
    columns = jnp.arange(face_order.shape[-1], dtype=jnp.int32)
    selector = (face_order[:, :, :, None] == columns[None, None, None, :]).astype(jnp.bfloat16)
    return jnp.einsum(
        "deri,deic->derc", face_couplings, selector, preferred_element_type=jnp.float32
    ).astype(jnp.bfloat16)


def apply_blocks(blocks, coupled, next_faces, padded):
    centre = padded[1:-1]
    total = jnp.einsum("xyzij,xyzjc->xyzic", blocks, centre, preferred_element_type=jnp.float32)
    total = total + jnp.einsum(
        "xyzij,xyzjc->xyzic", coupled[0], padded[:-2], preferred_element_type=jnp.float32
    )
    total = total + jnp.einsum(
        "xyzji,xyzjc->xyzic", next_faces, padded[2:], preferred_element_type=jnp.float32
    )
    for axis_number in (1, 2):
        faces = coupled[axis_number]
        before = jnp.roll(centre, 1, axis_number)
        after = jnp.roll(centre, -1, axis_number)
        faces_after = jnp.roll(faces, -1, axis_number)
        total = total + jnp.einsum(
            "xyzij,xyzjc->xyzic", faces, before, preferred_element_type=jnp.float32
        )
        total = total + jnp.einsum(
            "xyzji,xyzjc->xyzic", faces_after, after, preferred_element_type=jnp.float32
        )
    return total


def filter_scalars(energy, weight, total_count):
    energy, weight = sum_scalars(energy, weight)
    cut_level = energy / total_count / (weight / total_count + mean_epsilon)
    return ((spectrum_top + cut_level) * 0.5, (spectrum_top - cut_level) * 0.5)


def dot_split(a, b, dims):
    a_high = a.astype(jnp.bfloat16)
    a_low = (a - a_high.astype(jnp.float32)).astype(jnp.bfloat16)
    b_high = b.astype(jnp.bfloat16)
    b_low = (b - b_high.astype(jnp.float32)).astype(jnp.bfloat16)

    def part(x, y):
        return lax.dot_general(x, y, (dims, ((), ())), preferred_element_type=jnp.float32)

    return part(a_high, b_high) + (part(a_high, b_low) + part(a_low, b_high))


def inverse_factor(block):
    tiles = BLOCK // 8
    lane = lax.broadcasted_iota(jnp.int32, (1, BLOCK), 1)
    sub = lax.broadcasted_iota(jnp.int32, (8, 1), 0)

    def group(step, state):
        head = state[0]
        columns = [jnp.broadcast_to(head[:, j : j + 1], (8, BLOCK)) for j in range(8)]
        rows = jnp.where(lane < 8, jnp.where(lane == sub, 1.0, 0.0), head)
        for j in range(8):
            factor = jnp.where(sub > j, columns[j] * (1.0 / columns[j][j : j + 1, :]), 0.0)
            for k in range(j + 1, 8):
                columns[k] = columns[k] - factor * columns[k][j : j + 1, :]
            rows = rows - factor * rows[j : j + 1, :]
        pivots = columns[0]
        for j in range(1, 8):
            pivots = jnp.where(sub == j, columns[j], pivots)
        inverse = 1.0 / pivots
        solved = rows * inverse
        for j in range(7, 0, -1):
            factor = jnp.where(sub < j, columns[j] * inverse, 0.0)
            solved = solved - factor * solved[j : j + 1, :]
        result = []
        for t in range(1, tiles):
            new = jnp.where(lane < 8, 0.0, state[t])
            for j in range(8):
                new = new - state[t][:, j : j + 1] * solved[j : j + 1, :]
            result.append(jnp.where(t < tiles - step, new, state[t]))
        result.append(rows * lax.rsqrt(pivots))
        return tuple(pltpu.roll(x, BLOCK - 8, 1) for x in result)

    state = tuple(block[8 * t : 8 * t + 8, :] for t in range(tiles))
    state = lax.fori_loop(0, tiles, group, state, unroll=4)
    full = jnp.concatenate(state, axis=0)
    rows = lax.broadcasted_iota(jnp.int32, (BLOCK, BLOCK), 0)
    columns = lax.broadcasted_iota(jnp.int32, (BLOCK, BLOCK), 1)
    return jnp.where(columns <= rows, full, 0.0)


def partner_of(me, bit):
    distance = 1 << bit
    side = lax.rem(lax.div(me, distance), 2)
    return me + distance * (1 - 2 * side), side


def greet(axis, bits):
    me = lax.axis_index(axis)
    barrier = pltpu.get_barrier_semaphore()
    for bit in bits:
        other, _ = partner_of(me, bit)
        pl.semaphore_signal(
            barrier, inc=1, device_id={axis: other}, device_id_type=pl.DeviceIdType.MESH
        )
    pl.semaphore_wait(barrier, len(bits))
    return me


def scalar_sum_kernel(bits, own_ref, out_ref, held, landed, send_sem, recv_sem):
    me = greet("ex", bits)
    held[0] = own_ref[...]
    for step, bit in enumerate(bits):
        other, _ = partner_of(me, bit)
        copy = pltpu.make_async_remote_copy(
            src_ref=held.at[step],
            dst_ref=landed.at[step],
            send_sem=send_sem.at[step],
            recv_sem=recv_sem.at[step],
            device_id={"ex": other},
            device_id_type=pl.DeviceIdType.MESH,
        )
        copy.start()
        copy.wait()
        held[step + 1] = held[step] + landed[step]
    out_ref[...] = held[len(bits)]


def bits_of(axis):
    count = lax.axis_size(axis)
    return list(range(count.bit_length() - 1))


def sum_scalars(first, second):
    bits = bits_of("ex")
    rows = lax.broadcasted_iota(jnp.int32, (8, 128), 0)
    own = jnp.where(rows < 4, first, second)
    whole = pl.BlockSpec(memory_space=pltpu.VMEM)
    total = pl.pallas_call(
        functools.partial(scalar_sum_kernel, bits),
        out_shape=jax.ShapeDtypeStruct((8, 128), jnp.float32),
        in_specs=[whole],
        out_specs=whole,
        scratch_shapes=[
            pltpu.VMEM((len(bits) + 1, 8, 128), jnp.float32),
            pltpu.VMEM((len(bits), 8, 128), jnp.float32),
            pltpu.SemaphoreType.DMA((len(bits),)),
            pltpu.SemaphoreType.DMA((len(bits),)),
        ],
        compiler_params=pltpu.CompilerParams(collective_id=0, has_side_effects=True),
    )(own)
    return total[0, 0], total[4, 0]


def gram_sum_kernel(streams, gram_ref, out_ref, work, landed, send_sem, recv_sem):
    me = greet("ex", sorted(streams[0][2]))
    blocks = gram_ref.shape[0] // BLOCK
    place = 0
    for i in range(blocks):
        for j in range(i + 1):
            tile = gram_ref[i * BLOCK : (i + 1) * BLOCK, j * BLOCK : (j + 1) * BLOCK]
            work[place : place + BLOCK // 8] = tile.reshape(BLOCK // 8, 8, 128)
            place += BLOCK // 8
    steps = len(streams[0][2])
    offsets = [start for start, _, _ in streams]
    lengths = [length for _, length, _ in streams]
    landings = [start for start, _, _ in streams]

    def send(s, source, target, number, other):
        copy = pltpu.make_async_remote_copy(
            src_ref=source,
            dst_ref=target,
            send_sem=send_sem.at[s, number],
            recv_sem=recv_sem.at[s, number],
            device_id={"ex": other},
            device_id_type=pl.DeviceIdType.MESH,
        )
        copy.start()
        return copy

    def scatter(s, step):
        other, side = partner_of(me, streams[s][2][step])
        half = lengths[s] // 2
        given = offsets[s] + (1 - side) * half
        lengths[s] = half
        offsets[s] = offsets[s] + side * half
        landing = landings[s]
        landings[s] = landing + half
        copy = send(s, work.at[pl.ds(given, half)], landed.at[pl.ds(landing, half)], step, other)
        return copy, landing

    def gather(s, step):
        bit = streams[s][2][steps - 1 - step]
        other, side = partner_of(me, bit)
        here = pl.ds(offsets[s], lengths[s])
        copy = send(s, out_ref.at[here], out_ref.at[here], steps + step, other)
        offsets[s] = offsets[s] - side * lengths[s]
        lengths[s] = lengths[s] * 2
        return copy

    several = range(len(streams))
    flying = [scatter(s, 0) for s in several]
    for step in range(steps):
        for s in several:
            copy, landing = flying[s]
            copy.wait()
            kept = pl.ds(offsets[s], lengths[s])
            total = work[kept] + landed[landing : landing + lengths[s]]
            if step + 1 < steps:
                work[kept] = total
                flying[s] = scatter(s, step + 1)
            else:
                out_ref[kept] = total
                flying[s] = gather(s, 0)
    for step in range(steps):
        for s in several:
            flying[s].wait()
            if step + 1 < steps:
                flying[s] = gather(s, step + 1)


def sum_gram(gram):
    bits = bits_of("ex")
    count = lax.axis_size("ex")
    blocks = gram.shape[0] // BLOCK
    tiles = blocks * (blocks + 1) // 2 * (BLOCK // 8)
    cut = tiles // count // 2 * count
    streams = [(0, cut, bits), (cut, tiles - cut, bits[:1] + bits[2:] + bits[1:2])]
    whole = pl.BlockSpec(memory_space=pltpu.VMEM)
    return pl.pallas_call(
        functools.partial(gram_sum_kernel, streams),
        out_shape=jax.ShapeDtypeStruct((tiles, 8, 128), jnp.float32),
        in_specs=[whole],
        out_specs=whole,
        scratch_shapes=[
            pltpu.VMEM((tiles, 8, 128), jnp.float32),
            pltpu.VMEM((tiles, 8, 128), jnp.float32),
            pltpu.SemaphoreType.DMA((2, 2 * len(bits))),
            pltpu.SemaphoreType.DMA((2, 2 * len(bits))),
        ],
        compiler_params=pltpu.CompilerParams(
            collective_id=1, has_side_effects=True, vmem_limit_bytes=32 * 1024 * 1024
        ),
    )(gram)


def orthonormal_kernel(row_count, gram_ref, filtered_ref, out_ref, work):
    size = work.shape[0]
    place = 0
    for i in range(size // BLOCK):
        for j in range(i + 1):
            tile = gram_ref[place : place + BLOCK // 8].reshape(BLOCK, BLOCK)
            work[i * BLOCK : (i + 1) * BLOCK, j * BLOCK : (j + 1) * BLOCK] = tile * (1.0 / row_count)
            place += BLOCK // 8
    for start in range(0, size, BLOCK):
        stop = start + BLOCK
        inverse = inverse_factor(work[start:stop, start:stop])
        if start > 0:
            work[start:stop, :start] = dot_split(inverse, work[start:stop, :start], ((1,), (0,)))
        work[start:stop, start:stop] = inverse
        if stop < size:
            lower = dot_split(work[stop:, start:stop], inverse, ((1,), (1,)))
            work[start:stop, stop:] = lower.T
            work[stop:, start:stop] = jnp.zeros((size - stop, BLOCK), jnp.float32)
            for column in range(0, size, BLOCK):
                first = max(stop, column)
                work[first:, column : column + BLOCK] -= dot_split(
                    lower[first - stop :], work[start:stop, column : column + BLOCK], ((1,), (0,))
                )
    for start in range(0, size, 256):
        stop = start + 256
        rows = lax.broadcasted_iota(jnp.int32, (256, stop), 0) + start
        columns = lax.broadcasted_iota(jnp.int32, (256, stop), 1)
        wide = jnp.where(columns <= rows, work[start:stop, :stop], 0.0)
        high = wide.astype(jnp.bfloat16)
        low = (wide - high.astype(jnp.float32)).astype(jnp.bfloat16)
        total = lax.dot_general(
            filtered_ref[:, :stop], high, (((1,), (1,)), ((), ())),
            preferred_element_type=jnp.float32,
        )
        total = total + lax.dot_general(
            filtered_ref[:, :stop], low, (((1,), (1,)), ((), ())),
            preferred_element_type=jnp.float32,
        )
        out_ref[:, start:stop] = total.astype(jnp.bfloat16)


def orthonormalize(summed_gram, filtered, row_count):
    whole = pl.BlockSpec(memory_space=pltpu.VMEM)
    return pl.pallas_call(
        functools.partial(orthonormal_kernel, float(row_count)),
        out_shape=jax.ShapeDtypeStruct(filtered.shape, jnp.bfloat16),
        in_specs=[whole, whole],
        out_specs=whole,
        scratch_shapes=[pltpu.VMEM((filtered.shape[1],) * 2, jnp.float32)],
        compiler_params=pltpu.CompilerParams(vmem_limit_bytes=48 * 1024 * 1024),
    )(summed_gram, filtered)


def on_device(orbitals, element_blocks, face_couplings, face_order):
    local_rows, orbital_count = orbitals.shape
    elements = element_blocks.shape[0]
    basis_size = element_blocks.shape[1]
    layers = elements // (EY * EZ)
    slab_rows = EY * EZ * basis_size
    total_rows = local_rows * lax.axis_size("ex")
    total_count = float(total_rows * orbital_count)
    coupled = build_coupled(face_couplings, face_order).reshape(
        3, layers, EY, EZ, basis_size, basis_size
    )
    blocks = element_blocks.reshape(layers, EY, EZ, basis_size, basis_size)
    beyond = from_behind(coupled[0, 0], "ex", -1)
    next_faces = jnp.concatenate([coupled[0, 1:], beyond[None]], axis=0)
    chunk = orbital_count // CHUNKS

    def neighbour_product(values, sides):
        padded = jnp.concatenate([sides[0], values, sides[1]], axis=0)
        padded = padded.reshape(layers + 2, EY, EZ, basis_size, chunk)
        return apply_blocks(blocks, coupled, next_faces, padded).reshape(local_rows, chunk)

    starts = [orbitals[:, i * chunk : (i + 1) * chunk] for i in range(CHUNKS)]
    sides = [halo(starts[0], slab_rows)]
    for i in range(1, CHUNKS):
        sent, sides[i - 1] = lax.optimization_barrier((starts[i], sides[i - 1]))
        sides.append(halo(sent, slab_rows))
    products = [neighbour_product(*pair) for pair in zip(starts, sides)]
    energy = sum(jnp.sum(v.astype(jnp.float32) * p) for v, p in zip(starts, products))
    weight = jnp.sum(jnp.square(orbitals.astype(jnp.float32)))
    rounded = [p.astype(jnp.bfloat16) for p in products]
    before = sides[CHUNKS - 1]
    second_sides = []
    for i in range(CHUNKS):
        if i > 0:
            sent, before = lax.optimization_barrier((rounded[i], before))
            second_sides[i - 1] = before
        else:
            sent = rounded[i]
        before = halo(sent, slab_rows)
        second_sides.append(before)
    energy, weight, second_sides[0] = lax.optimization_barrier((energy, weight, second_sides[0]))
    center, half_width = filter_scalars(energy, weight, total_count)
    parts = []
    for value, product, narrow, beside in zip(starts, products, rounded, second_sides):
        wide = value.astype(jnp.float32)
        twice = neighbour_product(narrow, beside)
        second = (twice - center * narrow.astype(jnp.float32)) / half_width
        first = (product - center * wide) / half_width
        parts.append((2.0 * (second - center * first) / half_width - wide).astype(jnp.bfloat16))
    filtered = jnp.concatenate(parts, axis=1)
    summed_gram = sum_gram(
        jnp.einsum("rc,rd->cd", filtered, filtered, preferred_element_type=jnp.float32)
    )
    return orthonormalize(summed_gram, filtered, total_rows)


def solution(mesh):
    in_specs = (
        P(("groups", "ex"), None),
        P(("groups", "ex"), None, None),
        P(None, ("groups", "ex"), None, None),
        P(None, "ex", None),
    )
    out_specs = P(("groups", "ex"), None)
    return jax.shard_map(
        on_device, mesh=mesh, in_specs=in_specs, out_specs=out_specs, check_vma=False
    )
```
